32 devices in a mesh: dp: 16 (over z, y, core), expert: 2 (over x).
Axes of the slice: x: 2, y: 2, z: 4, core: 2. Of those that a mesh axis runs over, the one named last changes fastest.
Arguments:
- activations: bfloat16 [1024, 4096], P('expert', 'dp'), may hold values from -6 to 6
- out_grad: bfloat16 [1024, 4096], P('expert', 'dp'), may hold values from -6 to 6
- w_in: bfloat16 [2, 4096, 8192], P('expert', None, 'dp'), may hold values from -0.125 to 0.125
- w_out: bfloat16 [2, 8192, 4096], P('expert', 'dp'), may hold values from -0.0625 to 0.0625
- chosen: int32 [2, 256], replicated, may hold values from 0 to 1023, as said below
- gate_scores: float32 [2, 256], P('expert'), may hold values from 0.2 to 1
Outputs:
- w_in_grad: bfloat16 [2, 4096, 8192], P('expert', None, 'dp')
- w_out_grad: bfloat16 [2, 8192, 4096], P('expert', 'dp')
- act_grad: bfloat16 [1024, 4096], P('expert', 'dp')
- gate_grad: float32 [2, 256], P('expert')
The draws below stay inside these ranges and needn't reach their ends.
Inputs may be any that keep to these rules, and one draw needn't show every extreme that they name: Each row of chosen holds 256 distinct token numbers.
All inputs are finite; a program needn't handle non-finite values.
Results may differ from the reference program's by a relative error of at most 0.0075.
Values may be sent and summed in bfloat16 or wider, within the bound.
A program may use at most 64 MiB of HBM per device.

```python
import jax
import jax.numpy as jnp

D = 4096
FF = 8192
ROWS = 256
EXPERTS = 2
TOKENS = 1024


def draw_chosen(key, part):
    expert_keys = jax.random.split(key, EXPERTS)

    def one_list(expert_key):
        return jax.random.permutation(expert_key, TOKENS)[:ROWS]
    return jax.vmap(one_list)(expert_keys).astype(jnp.int32)


def spiked(array, key, source, target, blocks, factor):
    owner, partner = [(jnp.arange(array.shape[position]) // (array.shape[position] // blocks)).reshape([-1 if axis == position else 1 for axis in range(array.ndim)]) for position in (source, target)]
    chosen = jax.random.permutation(key, blocks)[partner]
    strong = (owner == chosen) | (owner == (partner + blocks // 2) % blocks)
    return jnp.where(strong, factor * array, array)


def block_scale(own_key, extent, shards, low, largest):
    def one(dim, parts):
        steps = jax.random.uniform(jax.random.fold_in(jax.random.fold_in(own_key, 6), dim), (parts,), jnp.float32, low / len(shards), largest / len(shards))
        return jnp.repeat(jnp.exp(steps), extent[dim] // parts).reshape((-1,) + (1,) * (len(extent) - dim - 1))

    factor_of = one(*shards[0])
    for cut in shards[1:]:
        factor_of = factor_of * one(*cut)
    return factor_of


def bell_draw(key, dims, width, reach, cuts=(), dtype=jnp.bfloat16):
    drawn = width * jax.random.normal(key, dims, jnp.float32)
    if cuts:
        drawn = drawn * block_scale(key, dims, cuts, -0.22, 0.18)
    return jnp.clip(drawn, -reach, reach).astype(dtype)


def heavy_noise(own_key, extent, spread, reach, cuts, heavy, held_as=jnp.bfloat16):
    result = spread * jax.random.normal(own_key, extent, jnp.float32)
    if cuts:
        result = result * block_scale(own_key, extent, cuts, -0.22, 0.18)
    return jnp.clip(spiked(result, jax.random.fold_in(own_key, 3), *heavy), -reach, reach).astype(held_as)


def setup_inputs(seed: int = 0) -> dict:
    key_list = jax.random.split(jax.random.key(seed), 7)
    return {
        "activations": bell_draw(key_list[0], (TOKENS, D), 1.0, 6.0, ((0, 2), (1, 16))),
        "out_grad": bell_draw(key_list[1], (TOKENS, D), 1.0, 6.0, ((0, 2), (1, 16))),
        "w_in": heavy_noise(key_list[2], (EXPERTS, D, FF), D ** -0.5, 0.125, ((0, 2), (2, 16)), (2, 1, 16, 2.0)),
        "w_out": bell_draw(key_list[3], (EXPERTS, FF, D), FF ** -0.5, 0.0625, ((0, 2), (1, 16))),
        "chosen": draw_chosen(jax.random.fold_in(key_list[6], 71), 0),
        "gate_scores": jnp.clip(0.2 + 0.8 * jax.random.uniform(key_list[5], (EXPERTS, ROWS), jnp.float32) ** block_scale(key_list[5], (EXPERTS, ROWS), ((0, 2),), -0.2, 0.2), 0.2, 1.0),
    }


GELU_SCALE = 0.7978845608
CUBIC_COEF = 0.044715


def gelu_parts(preact):
    inner = GELU_SCALE * (preact + CUBIC_COEF * preact * preact * preact)
    tanh_part = jnp.tanh(inner)
    gelu_val = 0.5 * preact * (1.0 + tanh_part)
    gelu_slope = 0.5 * (1.0 + tanh_part) + 0.5 * preact * (1.0 - tanh_part * tanh_part) * GELU_SCALE * (1.0 + 3.0 * CUBIC_COEF * preact * preact)
    return gelu_val, gelu_slope


def reference(activations, out_grad, w_in, w_out, chosen, gate_scores):
    act_total = jnp.zeros(activations.shape, jnp.float32)
    in_grads = []
    out_grads = []
    gate_rows = []
    for expert_id in range(EXPERTS):
        picked = chosen[expert_id].astype(jnp.int32)
        inputs = jnp.take(activations, picked, axis=0)
        upstream = jnp.take(out_grad, picked, axis=0)
        gated_grad = (gate_scores[expert_id][:, None] * upstream.astype(jnp.float32)).astype(jnp.bfloat16)
        preact = jnp.dot(inputs, w_in[expert_id], preferred_element_type=jnp.float32)
        gelu_val, gelu_slope = gelu_parts(preact)
        hidden = gelu_val.astype(jnp.bfloat16)
        raw_back = jnp.dot(upstream, w_out[expert_id].T, preferred_element_type=jnp.float32)
        gate_rows.append(jnp.sum(hidden.astype(jnp.float32) * raw_back, axis=1))
        hidden_back = jnp.dot(gated_grad, w_out[expert_id].T, preferred_element_type=jnp.float32)
        preact_back = (hidden_back * gelu_slope).astype(jnp.bfloat16)
        out_grads.append(jnp.dot(hidden.T, gated_grad, preferred_element_type=jnp.float32).astype(jnp.bfloat16))
        in_grads.append(jnp.dot(inputs.T, preact_back, preferred_element_type=jnp.float32).astype(jnp.bfloat16))
        input_back = jnp.dot(preact_back, w_in[expert_id].T, preferred_element_type=jnp.float32)
        act_total = act_total.at[picked].add(input_back)
    return (jnp.stack(in_grads), jnp.stack(out_grads), act_total.astype(jnp.bfloat16), jnp.stack(gate_rows))
```

```python
import jax
import jax.numpy as jnp
from jax import lax
from jax.experimental import pallas as pl
from jax.experimental.pallas import tpu as pltpu
from jax.sharding import PartitionSpec as P

GELU_SCALE = 0.7978845608
CUBIC_COEF = 0.044715


def gelu_parts(preact):
    inner = GELU_SCALE * (preact + CUBIC_COEF * preact * preact * preact)
    tanh_part = jnp.tanh(inner)
    gelu_val = 0.5 * preact * (1.0 + tanh_part)
    gelu_slope = 0.5 * (1.0 + tanh_part) + 0.5 * preact * (
        1.0 - tanh_part * tanh_part
    ) * GELU_SCALE * (1.0 + 3.0 * CUBIC_COEF * preact * preact)
    return (gelu_val, gelu_slope)


def contract(left_operand, right_operand, left_axis, right_axis):
    return lax.dot_general(
        left_operand,
        right_operand,
        (((left_axis,), (right_axis,)), ((), ())),
        preferred_element_type=jnp.float32,
    )


def exact_contract(left_operand, right_operand, left_axis, right_axis):
    return lax.dot_general(
        left_operand,
        right_operand,
        (((left_axis,), (right_axis,)), ((), ())),
        precision=lax.Precision.HIGHEST,
        preferred_element_type=jnp.float32,
    )


def input_sum(weight_in, preact_back):
    return lax.psum_scatter(
        contract(weight_in, preact_back, 1, 1), "dp", scatter_dimension=0, tiled=True
    )


def per_device(activations, out_grad, w_in, w_out, chosen, gate_scores):
    expert_id = lax.axis_index("expert")
    experts = lax.axis_size("expert")
    own_rows = activations.shape[0]
    every_act, every_grad = (
        lax.all_gather(activations, "expert", axis=0, tiled=True),
        lax.all_gather(out_grad, "expert", axis=0, tiled=True),
    )
    picked = lax.dynamic_index_in_dim(chosen, expert_id, 0, keepdims=False)
    inputs, upstream = (
        lax.all_gather(jnp.take(every_act, picked, axis=0), "dp", axis=1, tiled=True),
        lax.all_gather(jnp.take(every_grad, picked, axis=0), "dp", axis=1, tiled=True),
    )
    weight_in = w_in[0]
    weight_out = w_out[0]
    scores = gate_scores[0]
    gated_grad = (scores[:, None] * upstream.astype(jnp.float32)).astype(jnp.bfloat16)
    preact = jnp.dot(inputs, weight_in, preferred_element_type=jnp.float32)
    gelu_val, gelu_slope = gelu_parts(preact)
    hidden = gelu_val.astype(jnp.bfloat16)
    raw_back = contract(upstream, weight_out, 1, 1)
    gate_grad = lax.psum(jnp.sum(hidden.astype(jnp.float32) * raw_back, axis=1), "dp")
    hidden_back = contract(gated_grad, weight_out, 1, 1)
    preact_back = (hidden_back * gelu_slope).astype(jnp.bfloat16)
    weight_in_grad = contract(inputs, preact_back, 0, 0).astype(jnp.bfloat16)
    weight_out_grad = contract(hidden, gated_grad, 0, 0).astype(jnp.bfloat16)
    summed = input_sum(weight_in, preact_back)
    accumulated = jnp.zeros((summed.shape[0], own_rows), jnp.float32)
    expert_terms = lax.all_gather(summed[None], "expert", axis=0, tiled=True)
    token_ids = expert_id * own_rows + lax.iota(jnp.int32, own_rows)
    for expert_num in range(experts):
        onehot = (chosen[expert_num][None, :] == token_ids[:, None]).astype(jnp.float32)
        accumulated = accumulated + exact_contract(expert_terms[expert_num], onehot, 1, 1)
    act_grad = accumulated.T.astype(jnp.bfloat16)
    return (weight_in_grad[None], weight_out_grad[None], act_grad, gate_grad[None])

def flip(bit, with_bit):
    return bit + with_bit - 2 * bit * with_bit


def fused_kernel(
    act_ref, grad_ref, win_hbm, wout_hbm, chosen_ref, scores_ref,
    wing_hbm, woutg_hbm, actg_ref, gate_ref,
    win_v, wout_v, wing_v, woutg_v, gat, xsend, xrecv, pre, raw,
    hidden_t, back_b, gate_rows, part, s_send, s_recv, q_keep, y_send, y_recv,
    z_send, z_recv, t_send, t_recv, g_send, g_recv, local_sem, send_sem, recv_sem,
):
    me = lax.axis_index("dp")
    expert = lax.axis_index("expert")
    other = 1 - expert
    bits = [me % 2, (me // 2) % 2, (me // 4) % 2, (me // 8) % 2]
    own_rows, width = act_ref.shape
    rows = chosen_ref.shape[1]
    hidden_units = win_v.shape[1]
    zgroups = 4
    group_width = 4 * width

    def peer(mask):
        index = 0
        for place in range(4):
            bit = bits[place]
            index = index + (1 - bit if (mask >> place) & 1 else bit) * (1 << place)
        return {"dp": index}

    x_peer = {"expert": other}

    def group_of(kz):
        low = 1 - bits[2] if kz & 1 else bits[2]
        high = 1 - bits[3] if kz & 2 else bits[3]
        return low + 2 * high

    loads = [
        pltpu.make_async_copy(win_hbm.at[0], win_v, local_sem.at[0]),
        pltpu.make_async_copy(wout_hbm.at[0], wout_v, local_sem.at[1]),
    ]
    for load in loads:
        load.start()

    barrier = pltpu.get_barrier_semaphore()
    targets = [peer(1), peer(2), peer(4), peer(8), peer(12), x_peer]
    for target in targets:
        pl.semaphore_signal(
            barrier, inc=1, device_id=target, device_id_type=pl.DeviceIdType.MESH
        )

    token = expert * own_rows + lax.broadcasted_iota(jnp.int32, (own_rows, rows), 0)

    def onehot(which):
        picked = chosen_ref[pl.ds(which, 1), :]
        return jnp.where(picked == token, 1.0, 0.0).astype(jnp.bfloat16)

    own_hot = onehot(expert)
    other_hot = onehot(other)

    ids = {}

    def slot_of(key):
        return ids.setdefault(key, len(ids))

    started = []
    incoming = {}

    def send(source, landing, target, key):
        number = slot_of(key)
        copy = pltpu.make_async_remote_copy(
            src_ref=source,
            dst_ref=landing,
            send_sem=send_sem.at[number],
            recv_sem=recv_sem.at[number],
            device_id=target,
            device_id_type=pl.DeviceIdType.MESH,
        )
        copy.start()
        started.append(copy)
        incoming[key] = copy

    xsend[0] = contract(other_hot, act_ref[...], 0, 0).astype(jnp.bfloat16)
    pl.semaphore_wait(barrier, len(targets))
    send(xsend.at[0], xrecv.at[0], x_peer, ("x", 0))
    xsend[1] = contract(other_hot, grad_ref[...], 0, 0).astype(jnp.bfloat16)
    send(xsend.at[1], xrecv.at[1], x_peer, ("x", 1))
    own_picks = [
        contract(own_hot, ref[...], 0, 0).astype(jnp.bfloat16)
        for ref in (act_ref, grad_ref)
    ]
    pre[...] = jnp.zeros_like(pre)
    raw[...] = jnp.zeros_like(raw)

    def pass_on(array, k, mask):
        send(gat.at[array, k], gat.at[array, k ^ mask], peer(mask), ("g", array, k ^ mask))

    def arrived(array, k):
        incoming[("g", array, k)].wait_recv()

    def add_group(kz):
        base = group_of(kz)

        def body(step, carry):
            lane = flip(bits[0], step % 2) + 2 * flip(bits[1], step // 2)
            start = pl.multiple_of((4 * base + lane) * width, width)
            slot = 4 * kz + step
            pre[...] += jnp.dot(
                gat[0, slot], win_v[pl.ds(start, width), :],
                preferred_element_type=jnp.float32,
            )
            raw[...] += contract(gat[1, slot], wout_v[:, pl.ds(start, width)], 1, 1)
            return carry

        lax.fori_loop(0, 4, body, 0)

    for array in range(2):
        incoming[("x", array)].wait_recv()
        gat[array, 0] = own_picks[array] + xrecv[array]
        for mask in (4, 2, 8, 12, 1):
            pass_on(array, 0, mask)
    for load in loads:
        load.wait()
    for step in range(1, zgroups + 2):
        for array in range(2):
            if step < zgroups:
                arrived(array, 4 * step)
                pass_on(array, 4 * step, 2)
                pass_on(array, 4 * step, 1)
        for array in range(2):
            if step <= zgroups:
                arrived(array, 4 * (step - 1) + 2)
                pass_on(array, 4 * (step - 1) + 2, 1)
        if step >= 2:
            for array in range(2):
                arrived(array, 4 * (step - 2) + 1)
                arrived(array, 4 * (step - 2) + 3)
            add_group(step - 2)

    chunk = 32
    score_col = jnp.broadcast_to(scores_ref[...], (128, rows)).T
    gate_rows[...] = score_col

    def activate(step, carry):
        span = pl.ds(pl.multiple_of(step * chunk, chunk), chunk)
        gelu_val, gelu_slope = gelu_parts(pre[span, :])
        back = raw[span, :]
        score = jnp.concatenate([gate_rows[span, :]] * (hidden_units // 128), axis=1)
        hidden = gelu_val.astype(jnp.bfloat16).astype(jnp.float32)
        product = hidden * back
        folded = product[:, :128]
        for piece in range(1, hidden_units // 128):
            folded = folded + product[:, piece * 128:(piece + 1) * 128]
        back_b[span, :] = (score * back * gelu_slope).astype(jnp.bfloat16)
        pre[span, :] = score * gelu_val
        gate_rows[span, :] = folded
        return carry

    lax.fori_loop(0, rows // chunk, activate, 0)

    def partials(kz):
        base = group_of(kz)

        def body(step, carry):
            lane = flip(bits[0], step % 2) + 2 * flip(bits[1], step // 2)
            start = pl.multiple_of((4 * base + lane) * width, width)
            part[4 * kz + step] = contract(
                back_b[...], win_v[pl.ds(start, width), :], 1, 1
            )
            return carry

        lax.fori_loop(0, 4, body, 0)
        for ky in range(2):
            place = 2 * kz + ky
            s_send[place] = part[4 * kz + 2 * ky + 1].astype(jnp.bfloat16)
            send(s_send.at[place], s_recv.at[place], peer(1), ("s", place))

    def pair_sums(kz):
        place = 2 * kz + 1
        incoming[("s", place)].wait_recv()
        y_send[kz] = (part[4 * kz + 2] + s_recv[place].astype(jnp.float32)).astype(
            jnp.bfloat16
        )
        send(y_send.at[kz], y_recv.at[kz], peer(2), ("y", kz))
        incoming[("s", place - 1)].wait_recv()
        q_keep[kz] = part[4 * kz] + s_recv[place - 1].astype(jnp.float32)

    order = (2, 3, 1, 0)
    for position, kz in enumerate(order):
        partials(kz)
        if position:
            pair_sums(order[position - 1])
    pair_sums(order[-1])

    g_send[0] = jnp.broadcast_to(
        jnp.sum(gate_rows[...].T, axis=0, keepdims=True), (8, rows)
    )
    send(g_send.at[0], g_recv.at[0], peer(1), ("gate", 0))
    hidden_t[...] = pre[...].T.astype(jnp.bfloat16)

    stores = []

    def weight_grads(kz):
        base = group_of(kz)

        def body(step, carry):
            lane = flip(bits[0], step % 2) + 2 * flip(bits[1], step // 2)
            start = pl.multiple_of((4 * base + lane) * width, width)
            slot = 4 * kz + step
            wing_v[pl.ds(start, width), :] = contract(
                gat[0, slot], back_b[...], 0, 0
            ).astype(jnp.bfloat16)
            woutg_v[:, pl.ds(start, width)] = jnp.dot(
                hidden_t[...], gat[1, slot], preferred_element_type=jnp.float32
            ).astype(jnp.bfloat16)
            return carry

        lax.fori_loop(0, 4, body, 0)
        span = pl.ds(pl.multiple_of(base * group_width, group_width), group_width)
        for copy in (
            pltpu.make_async_copy(
                wing_v.at[span, :], wing_hbm.at[0, span, :], local_sem.at[2 + 2 * kz]
            ),
            pltpu.make_async_copy(
                woutg_v.at[:, span], woutg_hbm.at[0, :, span], local_sem.at[3 + 2 * kz]
            ),
        ):
            copy.start()
            stores.append(copy)

    weight_grads(0)
    incoming[("gate", 0)].wait_recv()
    g_send[1] = g_send[0] + g_recv[0]
    send(g_send.at[1], g_recv.at[1], peer(2), ("gate", 1))

    total = None
    for kz in order:
        incoming[("y", kz)].wait_recv()
        value = q_keep[kz] + y_recv[kz].astype(jnp.float32)
        if kz:
            z_send[kz - 1] = value.astype(jnp.bfloat16)
            send(z_send.at[kz - 1], z_recv.at[kz - 1], peer(4 * kz), ("z", kz - 1))
            if kz == order[0]:
                incoming[("gate", 1)].wait_recv()
                g_send[2] = g_send[1] + g_recv[1]
                for kg in range(1, zgroups):
                    send(g_send.at[2], g_recv.at[1 + kg], peer(4 * kg), ("gate", 1 + kg))
            weight_grads(kz)
        else:
            q_keep[0] = value
    total = q_keep[0]
    for kz in order[:-1]:
        incoming[("z", kz - 1)].wait_recv()
        total = total + z_recv[kz - 1].astype(jnp.float32)
    t_send[...] = total.astype(jnp.bfloat16)
    send(t_send, t_recv, x_peer, ("t", 0))
    for kg in range(1, zgroups):
        incoming[("gate", 1 + kg)].wait_recv()
    gate_sum = (g_send[2] + g_recv[2]) + (g_recv[3] + g_recv[4])
    gate_ref[...] = gate_sum[0:1, :]
    mine = jnp.dot(own_hot, t_send[...], preferred_element_type=jnp.float32)
    incoming[("t", 0)].wait_recv()
    theirs = jnp.dot(other_hot, t_recv[...], preferred_element_type=jnp.float32)
    actg_ref[...] = (mine + theirs).astype(jnp.bfloat16)
    for copy in stores:
        copy.wait()
    for copy in started:
        copy.wait_send()


def fused(activations, out_grad, w_in, w_out, chosen, gate_scores):
    own_rows, width = activations.shape
    _, model, hidden_units = w_in.shape
    rows = chosen.shape[1]
    copies = 64
    half, full = jnp.bfloat16, jnp.float32
    vmem = pl.BlockSpec(memory_space=pltpu.VMEM)
    anywhere = pl.BlockSpec(memory_space=pl.ANY)
    return pl.pallas_call(
        fused_kernel,
        out_shape=(
            jax.ShapeDtypeStruct((1, model, hidden_units), half),
            jax.ShapeDtypeStruct((1, hidden_units, model), half),
            jax.ShapeDtypeStruct((own_rows, width), half),
            jax.ShapeDtypeStruct((1, rows), full),
        ),
        in_specs=[vmem, vmem, anywhere, anywhere, vmem, vmem],
        out_specs=(anywhere, anywhere, vmem, vmem),
        scratch_shapes=[
            pltpu.VMEM((model, hidden_units), half),
            pltpu.VMEM((hidden_units, model), half),
            pltpu.VMEM((model, hidden_units), half),
            pltpu.VMEM((hidden_units, model), half),
            pltpu.VMEM((2, 16, rows, width), half),
            pltpu.VMEM((2, rows, width), half),
            pltpu.VMEM((2, rows, width), half),
            pltpu.VMEM((rows, hidden_units), full),
            pltpu.VMEM((rows, hidden_units), full),
            pltpu.VMEM((hidden_units, rows), half),
            pltpu.VMEM((rows, hidden_units), half),
            pltpu.VMEM((rows, 128), full),
            pltpu.VMEM((16, rows, width), full),
            pltpu.VMEM((8, rows, width), half),
            pltpu.VMEM((8, rows, width), half),
            pltpu.VMEM((4, rows, width), full),
            pltpu.VMEM((4, rows, width), half),
            pltpu.VMEM((4, rows, width), half),
            pltpu.VMEM((3, rows, width), half),
            pltpu.VMEM((3, rows, width), half),
            pltpu.VMEM((rows, width), half),
            pltpu.VMEM((rows, width), half),
            pltpu.VMEM((3, 8, rows), full),
            pltpu.VMEM((5, 8, rows), full),
            pltpu.SemaphoreType.DMA((10,)),
            pltpu.SemaphoreType.DMA((copies,)),
            pltpu.SemaphoreType.DMA((copies,)),
        ],
        compiler_params=pltpu.CompilerParams(
            collective_id=0, has_side_effects=True, vmem_limit_bytes=52 * 2**20
        ),
        cost_estimate=pl.CostEstimate(
            flops=10 * rows * model * hidden_units,
            bytes_accessed=8 * model * hidden_units,
            transcendentals=rows * hidden_units,
        ),
    )(activations, out_grad, w_in, w_out, chosen, gate_scores)


def fits(mesh, operands):
    activations, _, w_in, _, chosen, _ = operands
    return (
        mesh.shape["dp"] == 16
        and mesh.shape["expert"] == 2
        and activations.shape[0] % 256 == 0
        and activations.shape[1] == 4096
        and w_in.shape == (2, 4096, 8192)
        and chosen.shape == (2, 256)
    )


def solution(mesh):
    def run(*operands):
        body = fused if fits(mesh, operands) else per_device
        return jax.shard_map(
            body,
            mesh=mesh,
            in_specs=(
                P("expert", "dp"),
                P("expert", "dp"),
                P("expert", None, "dp"),
                P("expert", "dp", None),
                P(),
                P("expert", None),
            ),
            out_specs=(
                P("expert", None, "dp"),
                P("expert", "dp", None),
                P("expert", "dp"),
                P("expert", None),
            ),
            check_vma=False,
        )(*operands)

    return run
```

```python
import jax
import jax.numpy as jnp
from jax import lax
from jax.experimental import pallas as pl
from jax.experimental.pallas import tpu as pltpu
from jax.sharding import PartitionSpec as P

GELU_SCALE = 0.7978845608
CUBIC_COEF = 0.044715


def gelu_parts(preact):
    inner = GELU_SCALE * (preact + CUBIC_COEF * preact * preact * preact)
    tanh_part = jnp.tanh(inner)
    gelu_val = 0.5 * preact * (1.0 + tanh_part)
    gelu_slope = 0.5 * (1.0 + tanh_part) + 0.5 * preact * (
        1.0 - tanh_part * tanh_part
    ) * GELU_SCALE * (1.0 + 3.0 * CUBIC_COEF * preact * preact)
    return (gelu_val, gelu_slope)


def contract(left_operand, right_operand, left_axis, right_axis):
    return lax.dot_general(
        left_operand,
        right_operand,
        (((left_axis,), (right_axis,)), ((), ())),
        preferred_element_type=jnp.float32,
    )


def exact_contract(left_operand, right_operand, left_axis, right_axis):
    return lax.dot_general(
        left_operand,
        right_operand,
        (((left_axis,), (right_axis,)), ((), ())),
        precision=lax.Precision.HIGHEST,
        preferred_element_type=jnp.float32,
    )


def input_sum(weight_in, preact_back):
    return lax.psum_scatter(
        contract(weight_in, preact_back, 1, 1), "dp", scatter_dimension=0, tiled=True
    )


def per_device(activations, out_grad, w_in, w_out, chosen, gate_scores):
    expert_id = lax.axis_index("expert")
    experts = lax.axis_size("expert")
    own_rows = activations.shape[0]
    every_act, every_grad = (
        lax.all_gather(activations, "expert", axis=0, tiled=True),
        lax.all_gather(out_grad, "expert", axis=0, tiled=True),
    )
    picked = lax.dynamic_index_in_dim(chosen, expert_id, 0, keepdims=False)
    inputs, upstream = (
        lax.all_gather(jnp.take(every_act, picked, axis=0), "dp", axis=1, tiled=True),
        lax.all_gather(jnp.take(every_grad, picked, axis=0), "dp", axis=1, tiled=True),
    )
    weight_in = w_in[0]
    weight_out = w_out[0]
    scores = gate_scores[0]
    gated_grad = (scores[:, None] * upstream.astype(jnp.float32)).astype(jnp.bfloat16)
    preact = jnp.dot(inputs, weight_in, preferred_element_type=jnp.float32)
    gelu_val, gelu_slope = gelu_parts(preact)
    hidden = gelu_val.astype(jnp.bfloat16)
    raw_back = contract(upstream, weight_out, 1, 1)
    gate_grad = lax.psum(jnp.sum(hidden.astype(jnp.float32) * raw_back, axis=1), "dp")
    hidden_back = contract(gated_grad, weight_out, 1, 1)
    preact_back = (hidden_back * gelu_slope).astype(jnp.bfloat16)
    weight_in_grad = contract(inputs, preact_back, 0, 0).astype(jnp.bfloat16)
    weight_out_grad = contract(hidden, gated_grad, 0, 0).astype(jnp.bfloat16)
    summed = input_sum(weight_in, preact_back)
    accumulated = jnp.zeros((summed.shape[0], own_rows), jnp.float32)
    expert_terms = lax.all_gather(summed[None], "expert", axis=0, tiled=True)
    token_ids = expert_id * own_rows + lax.iota(jnp.int32, own_rows)
    for expert_num in range(experts):
        onehot = (chosen[expert_num][None, :] == token_ids[:, None]).astype(jnp.float32)
        accumulated = accumulated + exact_contract(expert_terms[expert_num], onehot, 1, 1)
    act_grad = accumulated.T.astype(jnp.bfloat16)
    return (weight_in_grad[None], weight_out_grad[None], act_grad, gate_grad[None])

def flip(bit, with_bit):
    return bit + with_bit - 2 * bit * with_bit


def fused_kernel(
    act_hbm, grad_hbm, win_hbm, wout_hbm, chosen_hbm, scores_hbm,
    wing_v, woutg_v, actg_ref, gate_ref,
    act_ref, grad_ref, chosen_ref, scores_ref, win_v, wout_v, gat, xsend, xrecv, pre, raw,
    hidden_t, back_b, gate_rows, part, s_send, s_recv, q_keep, y_send, y_recv,
    z_send, z_recv, t_send, t_recv, g_send, g_recv, local_sem, send_sem, recv_sem, gather_sem,
):
    me = lax.axis_index("dp")
    expert = lax.axis_index("expert")
    other = 1 - expert
    bits = [me % 2, (me // 2) % 2, (me // 4) % 2, (me // 8) % 2]
    own_rows, width = act_ref.shape
    rows = chosen_ref.shape[1]
    hidden_units = win_v.shape[1]
    zgroups = 4

    def peer(mask):
        index = 0
        for place in range(4):
            bit = bits[place]
            index = index + (1 - bit if (mask >> place) & 1 else bit) * (1 << place)
        return {"dp": index}

    x_peer = {"expert": other}

    def group_of(kz):
        return flip(bits[2], kz % 2) + 2 * flip(bits[3], kz // 2)

    loads = [
        pltpu.make_async_copy(source, landing, local_sem.at[number])
        for number, (source, landing) in enumerate(
            (
                (chosen_hbm, chosen_ref),
                (act_hbm, act_ref),
                (grad_hbm, grad_ref),
                (scores_hbm, scores_ref),
                (win_hbm.at[0], win_v),
                (wout_hbm.at[0], wout_v),
            )
        )
    ]
    for load in loads:
        load.start()

    barrier = pltpu.get_barrier_semaphore()
    targets = [x_peer, peer(1), peer(2), peer(4), peer(8), peer(12)]
    for target in targets:
        pl.semaphore_signal(
            barrier, inc=1, device_id=target, device_id_type=pl.DeviceIdType.MESH
        )

    token = expert * own_rows + lax.broadcasted_iota(jnp.int32, (own_rows, rows), 0)

    def onehot(which):
        picked = chosen_ref[pl.ds(which, 1), :]
        return jnp.where(picked == token, 1.0, 0.0).astype(jnp.bfloat16)

    loads[0].wait()
    other_hot = onehot(other)
    own_hot = onehot(expert)

    ids = {}

    def slot_of(key):
        return ids.setdefault(key, len(ids))

    started = []
    incoming = {}

    def send(source, landing, target, key):
        number = slot_of(key)
        copy = pltpu.make_async_remote_copy(
            src_ref=source,
            dst_ref=landing,
            send_sem=send_sem.at[number],
            recv_sem=recv_sem.at[number],
            device_id=target,
            device_id_type=pl.DeviceIdType.MESH,
        )
        copy.start()
        started.append(copy)
        incoming[key] = copy

    loads[1].wait()
    xsend[0] = contract(other_hot, act_ref[...], 0, 0).astype(jnp.bfloat16)
    pl.semaphore_wait(barrier, len(targets))
    send(xsend.at[0], xrecv.at[0], x_peer, ("x", 0))
    loads[2].wait()
    xsend[1] = contract(other_hot, grad_ref[...], 0, 0).astype(jnp.bfloat16)
    send(xsend.at[1], xrecv.at[1], x_peer, ("x", 1))
    own_picks = [
        contract(own_hot, ref[...], 0, 0).astype(jnp.bfloat16)
        for ref in (act_ref, grad_ref)
    ]
    pre[...] = jnp.zeros_like(pre)
    raw[...] = jnp.zeros_like(raw)

    inner = flip(bits[2], bits[3])
    by_inner = []

    def pass_on(array, slot, landing, target, key):
        copy = pltpu.make_async_remote_copy(
            src_ref=gat.at[array, slot],
            dst_ref=gat.at[array, landing],
            send_sem=send_sem.at[slot_of(("g", array) + key)],
            recv_sem=gather_sem.at[array, landing],
            device_id=target,
            device_id_type=pl.DeviceIdType.MESH,
        )
        return copy

    def begin(copy):
        copy.start()
        started.append(copy)

    def arrived(array, slot):
        pltpu.make_async_remote_copy(
            src_ref=gat.at[array, slot],
            dst_ref=gat.at[array, slot],
            send_sem=send_sem.at[0],
            recv_sem=gather_sem.at[array, slot],
            device_id=peer(1),
            device_id_type=pl.DeviceIdType.MESH,
        ).wait_recv()

    def to_pair(array, kz, low, step):
        begin(
            pass_on(array, 4 * kz + low, 4 * kz + low + 1, peer(1), ("pair", step, low))
        )

    def to_column(array, kz, step):
        begin(
            pass_on(array, 4 * kz, 4 * kz + 2, peer(2), ("column", step))
        )

    def along_line(array, slot, landing, mask, step):
        copy = pass_on(array, slot, landing, peer(mask), ("line", step))
        by_inner.append(copy)

        @pl.when(inner == 1)
        def _():
            copy.start()

    def add_group(kz):
        base = group_of(kz)

        def body(step, carry):
            lane = flip(bits[0], step % 2) + 2 * flip(bits[1], step // 2)
            start = pl.multiple_of((4 * base + lane) * width, width)
            slot = 4 * kz + step
            pre[...] += jnp.dot(
                gat[0, slot], win_v[pl.ds(start, width), :],
                preferred_element_type=jnp.float32,
            )
            raw[...] += contract(gat[1, slot], wout_v[:, pl.ds(start, width)], 1, 1)
            return carry

        lax.fori_loop(0, 4, body, 0)

    kz_at = [0, 1, 2 + inner, 3 - inner]
    for array in range(2):
        incoming[("x", array)].wait_recv()
        gat[array, 0] = own_picks[array] + xrecv[array]
        begin(pass_on(array, 0, 4, peer(4), ("own",)))
        along_line(array, 0, 12, 12, 0)
        to_column(array, 0, 0)
        to_pair(array, 0, 0, 0)
    for load in loads[3:]:
        load.wait()
    for step in range(1, zgroups + 2):
        for array in range(2):
            if step < zgroups:
                kz = kz_at[step]
                arrived(array, 4 * kz)
                if step == 1:
                    along_line(array, 4, 8, 12, 1)
                elif step == 2:
                    along_line(array, 12, 8, 4, 2)
                else:
                    along_line(array, 8, 12, 4, 3)
                to_column(array, kz, step)
                to_pair(array, kz, 0, step)
        for array in range(2):
            if step <= zgroups:
                kz = kz_at[step - 1]
                arrived(array, 4 * kz + 2)
                to_pair(array, kz, 2, step - 1)
        if step >= 2:
            kz = kz_at[step - 2]
            for array in range(2):
                arrived(array, 4 * kz + 1)
                arrived(array, 4 * kz + 3)
            add_group(kz)

    chunk = 32
    score_col = jnp.broadcast_to(scores_ref[...], (128, rows)).T
    gate_rows[...] = score_col

    def activate(step, carry):
        span = pl.ds(pl.multiple_of(step * chunk, chunk), chunk)
        gelu_val, gelu_slope = gelu_parts(pre[span, :])
        back = raw[span, :]
        score = jnp.concatenate([gate_rows[span, :]] * (hidden_units // 128), axis=1)
        hidden = gelu_val.astype(jnp.bfloat16).astype(jnp.float32)
        product = hidden * back
        folded = product[:, :128]
        for piece in range(1, hidden_units // 128):
            folded = folded + product[:, piece * 128:(piece + 1) * 128]
        back_b[span, :] = (score * back * gelu_slope).astype(jnp.bfloat16)
        pre[span, :] = score * gelu_val
        gate_rows[span, :] = folded
        return carry

    lax.fori_loop(0, rows // chunk, activate, 0)

    def partials(kz):
        base = group_of(kz)

        def body(step, carry):
            lane = flip(bits[0], step % 2) + 2 * flip(bits[1], step // 2)
            start = pl.multiple_of((4 * base + lane) * width, width)
            part[4 * kz + step] = contract(
                back_b[...], win_v[pl.ds(start, width), :], 1, 1
            )
            return carry

        lax.fori_loop(0, 4, body, 0)
        for ky in range(2):
            place = 2 * kz + ky
            s_send[place] = part[4 * kz + 2 * ky + 1].astype(jnp.bfloat16)
            send(s_send.at[place], s_recv.at[place], peer(1), ("s", place))

    def pair_sums(kz):
        place = 2 * kz + 1
        incoming[("s", place)].wait_recv()
        y_send[kz] = (part[4 * kz + 2] + s_recv[place].astype(jnp.float32)).astype(
            jnp.bfloat16
        )
        send(y_send.at[kz], y_recv.at[kz], peer(2), ("y", kz))
        incoming[("s", place - 1)].wait_recv()
        q_keep[kz] = part[4 * kz] + s_recv[place - 1].astype(jnp.float32)

    order = (2, 3, 1, 0)
    for position, kz in enumerate(order):
        partials(kz)
        if position:
            pair_sums(order[position - 1])
    pair_sums(order[-1])

    g_send[0] = jnp.broadcast_to(
        jnp.sum(gate_rows[...].T, axis=0, keepdims=True), (8, rows)
    )
    send(g_send.at[0], g_recv.at[0], peer(1), ("gate", 0))
    hidden_t[...] = pre[...].T.astype(jnp.bfloat16)

    def weight_grads(kz):
        base = group_of(kz)

        def body(step, carry):
            lane = flip(bits[0], step % 2) + 2 * flip(bits[1], step // 2)
            start = pl.multiple_of((4 * base + lane) * width, width)
            slot = 4 * kz + step
            wing_v[pl.ds(start, width), :] = contract(
                gat[0, slot], back_b[...], 0, 0
            ).astype(jnp.bfloat16)
            woutg_v[:, pl.ds(start, width)] = jnp.dot(
                hidden_t[...], gat[1, slot], preferred_element_type=jnp.float32
            ).astype(jnp.bfloat16)
            return carry

        lax.fori_loop(0, 4, body, 0)

    weight_grads(0)
    incoming[("gate", 0)].wait_recv()
    g_send[1] = g_send[0] + g_recv[0]
    send(g_send.at[1], g_recv.at[1], peer(2), ("gate", 1))

    total = None
    for kz in order:
        incoming[("y", kz)].wait_recv()
        value = q_keep[kz] + y_recv[kz].astype(jnp.float32)
        if kz:
            z_send[kz - 1] = value.astype(jnp.bfloat16)
            send(z_send.at[kz - 1], z_recv.at[kz - 1], peer(4 * kz), ("z", kz - 1))
            if kz == order[0]:
                incoming[("gate", 1)].wait_recv()
                g_send[2] = g_send[1] + g_recv[1]
                for kg in range(1, zgroups):
                    send(g_send.at[2], g_recv.at[1 + kg], peer(4 * kg), ("gate", 1 + kg))
            weight_grads(kz)
        else:
            q_keep[0] = value
    total = q_keep[0]
    for kz in order[:-1]:
        incoming[("z", kz - 1)].wait_recv()
        total = total + z_recv[kz - 1].astype(jnp.float32)
    t_send[...] = total.astype(jnp.bfloat16)
    send(t_send, t_recv, x_peer, ("t", 0))
    for kg in range(1, zgroups):
        incoming[("gate", 1 + kg)].wait_recv()
    gate_sum = (g_send[2] + g_recv[2]) + (g_recv[3] + g_recv[4])
    gate_ref[...] = gate_sum[0:1, :]
    mine = jnp.dot(own_hot, t_send[...], preferred_element_type=jnp.float32)
    incoming[("t", 0)].wait_recv()
    theirs = jnp.dot(other_hot, t_recv[...], preferred_element_type=jnp.float32)
    actg_ref[...] = (mine + theirs).astype(jnp.bfloat16)
    for copy in started:
        copy.wait_send()

    @pl.when(inner == 1)
    def _():
        for copy in by_inner:
            copy.wait_send()


def store_kernel(*refs):
    sources, results, sems = refs[:4], refs[4:8], refs[8]
    pieces = 4
    copies = []
    for place in range(2):
        source, result = sources[place], results[place].at[0]
        step = source.shape[0] // pieces
        for piece in range(pieces):
            span = pl.ds(piece * step, step)
            copies.append((source.at[span], result.at[span]))
    copies += [(sources[place], results[place]) for place in (2, 3)]
    running = [
        pltpu.make_async_copy(source, result, sems.at[number])
        for number, (source, result) in enumerate(copies)
    ]
    for copy in running:
        copy.start()
    for copy in running:
        copy.wait()


def fused(activations, out_grad, w_in, w_out, chosen, gate_scores):
    own_rows, width = activations.shape
    _, model, hidden_units = w_in.shape
    rows = chosen.shape[1]
    copies = 64
    half, full = jnp.bfloat16, jnp.float32
    vmem = pl.BlockSpec(memory_space=pltpu.VMEM)
    in_hbm = pl.BlockSpec(memory_space=pltpu.HBM)
    results = pl.pallas_call(
        fused_kernel,
        out_shape=(
            jax.ShapeDtypeStruct((model, hidden_units), half),
            jax.ShapeDtypeStruct((hidden_units, model), half),
            jax.ShapeDtypeStruct((own_rows, width), half),
            jax.ShapeDtypeStruct((1, rows), full),
        ),
        in_specs=[in_hbm] * 6,
        out_specs=(vmem,) * 4,
        scratch_shapes=[
            pltpu.VMEM((own_rows, width), half),
            pltpu.VMEM((own_rows, width), half),
            pltpu.VMEM(chosen.shape, chosen.dtype),
            pltpu.VMEM((1, rows), full),
            pltpu.VMEM((model, hidden_units), half),
            pltpu.VMEM((hidden_units, model), half),
            pltpu.VMEM((2, 16, rows, width), half),
            pltpu.VMEM((2, rows, width), half),
            pltpu.VMEM((2, rows, width), half),
            pltpu.VMEM((rows, hidden_units), full),
            pltpu.VMEM((rows, hidden_units), full),
            pltpu.VMEM((hidden_units, rows), half),
            pltpu.VMEM((rows, hidden_units), half),
            pltpu.VMEM((rows, 128), full),
            pltpu.VMEM((16, rows, width), full),
            pltpu.VMEM((8, rows, width), half),
            pltpu.VMEM((8, rows, width), half),
            pltpu.VMEM((4, rows, width), full),
            pltpu.VMEM((4, rows, width), half),
            pltpu.VMEM((4, rows, width), half),
            pltpu.VMEM((3, rows, width), half),
            pltpu.VMEM((3, rows, width), half),
            pltpu.VMEM((rows, width), half),
            pltpu.VMEM((rows, width), half),
            pltpu.VMEM((3, 8, rows), full),
            pltpu.VMEM((5, 8, rows), full),
            pltpu.SemaphoreType.DMA((10,)),
            pltpu.SemaphoreType.DMA((copies,)),
            pltpu.SemaphoreType.DMA((copies,)),
            pltpu.SemaphoreType.DMA((2, 16)),
        ],
        compiler_params=pltpu.CompilerParams(
            collective_id=0, has_side_effects=True, vmem_limit_bytes=44 * 2**20
        ),
        cost_estimate=pl.CostEstimate(
            flops=10 * rows * model * hidden_units,
            bytes_accessed=8 * model * hidden_units,
            transcendentals=rows * hidden_units,
        ),
    )(activations, out_grad, w_in, w_out, chosen, gate_scores)
    return pl.pallas_call(
        store_kernel,
        out_shape=(
            jax.ShapeDtypeStruct((1, model, hidden_units), half),
            jax.ShapeDtypeStruct((1, hidden_units, model), half),
            jax.ShapeDtypeStruct((own_rows, width), half),
            jax.ShapeDtypeStruct((1, rows), full),
        ),
        in_specs=[vmem] * 4,
        out_specs=(in_hbm,) * 4,
        scratch_shapes=[pltpu.SemaphoreType.DMA((10,))],
    )(*results)


def fits(mesh, operands):
    activations, _, w_in, _, chosen, _ = operands
    return (
        mesh.shape["dp"] == 16
        and mesh.shape["expert"] == 2
        and activations.shape[0] % 256 == 0
        and activations.shape[1] == 4096
        and w_in.shape == (2, 4096, 8192)
        and chosen.shape == (2, 256)
    )


def solution(mesh):
    def run(*operands):
        body = fused if fits(mesh, operands) else per_device
        return jax.shard_map(
            body,
            mesh=mesh,
            in_specs=(
                P("expert", "dp"),
                P("expert", "dp"),
                P("expert", None, "dp"),
                P("expert", "dp", None),
                P(),
                P("expert", None),
            ),
            out_specs=(
                P("expert", None, "dp"),
                P("expert", "dp", None),
                P("expert", "dp"),
                P("expert", None),
            ),
            check_vma=False,
        )(*operands)

    return run
```

```python
import jax
import jax.numpy as jnp
from jax import lax
from jax.experimental import pallas as pl
from jax.experimental.pallas import tpu as pltpu
from jax.sharding import PartitionSpec as P

GELU_SCALE = 0.7978845608
CUBIC_COEF = 0.044715


def gelu_parts(preact):
    inner = GELU_SCALE * (preact + CUBIC_COEF * preact * preact * preact)
    tanh_part = jnp.tanh(inner)
    gelu_val = 0.5 * preact * (1.0 + tanh_part)
    gelu_slope = 0.5 * (1.0 + tanh_part) + 0.5 * preact * (
        1.0 - tanh_part * tanh_part
    ) * GELU_SCALE * (1.0 + 3.0 * CUBIC_COEF * preact * preact)
    return (gelu_val, gelu_slope)


def contract(left_operand, right_operand, left_axis, right_axis):
    return lax.dot_general(
        left_operand,
        right_operand,
        (((left_axis,), (right_axis,)), ((), ())),
        preferred_element_type=jnp.float32,
    )


def exact_contract(left_operand, right_operand, left_axis, right_axis):
    return lax.dot_general(
        left_operand,
        right_operand,
        (((left_axis,), (right_axis,)), ((), ())),
        precision=lax.Precision.HIGHEST,
        preferred_element_type=jnp.float32,
    )


def input_sum(weight_in, preact_back):
    return lax.psum_scatter(
        contract(weight_in, preact_back, 1, 1), "dp", scatter_dimension=0, tiled=True
    )


def per_device(activations, out_grad, w_in, w_out, chosen, gate_scores):
    expert_id = lax.axis_index("expert")
    experts = lax.axis_size("expert")
    own_rows = activations.shape[0]
    every_act, every_grad = (
        lax.all_gather(activations, "expert", axis=0, tiled=True),
        lax.all_gather(out_grad, "expert", axis=0, tiled=True),
    )
    picked = lax.dynamic_index_in_dim(chosen, expert_id, 0, keepdims=False)
    inputs, upstream = (
        lax.all_gather(jnp.take(every_act, picked, axis=0), "dp", axis=1, tiled=True),
        lax.all_gather(jnp.take(every_grad, picked, axis=0), "dp", axis=1, tiled=True),
    )
    weight_in = w_in[0]
    weight_out = w_out[0]
    scores = gate_scores[0]
    gated_grad = (scores[:, None] * upstream.astype(jnp.float32)).astype(jnp.bfloat16)
    preact = jnp.dot(inputs, weight_in, preferred_element_type=jnp.float32)
    gelu_val, gelu_slope = gelu_parts(preact)
    hidden = gelu_val.astype(jnp.bfloat16)
    raw_back = contract(upstream, weight_out, 1, 1)
    gate_grad = lax.psum(jnp.sum(hidden.astype(jnp.float32) * raw_back, axis=1), "dp")
    hidden_back = contract(gated_grad, weight_out, 1, 1)
    preact_back = (hidden_back * gelu_slope).astype(jnp.bfloat16)
    weight_in_grad = contract(inputs, preact_back, 0, 0).astype(jnp.bfloat16)
    weight_out_grad = contract(hidden, gated_grad, 0, 0).astype(jnp.bfloat16)
    summed = input_sum(weight_in, preact_back)
    accumulated = jnp.zeros((summed.shape[0], own_rows), jnp.float32)
    expert_terms = lax.all_gather(summed[None], "expert", axis=0, tiled=True)
    token_ids = expert_id * own_rows + lax.iota(jnp.int32, own_rows)
    for expert_num in range(experts):
        onehot = (chosen[expert_num][None, :] == token_ids[:, None]).astype(jnp.float32)
        accumulated = accumulated + exact_contract(expert_terms[expert_num], onehot, 1, 1)
    act_grad = accumulated.T.astype(jnp.bfloat16)
    return (weight_in_grad[None], weight_out_grad[None], act_grad, gate_grad[None])

def flip(bit, with_bit):
    return bit + with_bit - 2 * bit * with_bit


def fused_kernel(
    act_hbm, grad_hbm, win_hbm, wout_hbm, chosen_hbm, scores_hbm,
    wing_v, woutg_v, actg_ref, gate_ref,
    act_ref, grad_ref, chosen_ref, scores_ref, win_v, wout_v, gat, xsend, xrecv, pre, raw,
    hidden_t, back_b, gate_rows, part, s_send, s_recv, q_keep, y_send, y_recv,
    z_send, z_recv, t_send, t_recv, g_send, g_recv, local_sem, send_sem, recv_sem, gather_sem,
):
    me = lax.axis_index("dp")
    expert = lax.axis_index("expert")
    other = 1 - expert
    bits = [me % 2, (me // 2) % 2, (me // 4) % 2, (me // 8) % 2]
    own_rows, width = act_ref.shape
    rows = chosen_ref.shape[1]
    hidden_units = win_v.shape[1]
    zgroups = 4

    def peer(mask):
        index = 0
        for place in range(4):
            bit = bits[place]
            index = index + (1 - bit if (mask >> place) & 1 else bit) * (1 << place)
        return {"dp": index}

    x_peer = {"expert": other}

    def group_of(kz):
        return flip(bits[2], kz % 2) + 2 * flip(bits[3], kz // 2)

    loads = [
        pltpu.make_async_copy(source, landing, local_sem.at[number])
        for number, (source, landing) in enumerate(
            (
                (chosen_hbm, chosen_ref),
                (act_hbm, act_ref),
                (grad_hbm, grad_ref),
                (scores_hbm, scores_ref),
                (win_hbm.at[0], win_v),
                (wout_hbm.at[0], wout_v),
            )
        )
    ]
    for load in loads:
        load.start()

    barrier = pltpu.get_barrier_semaphore()
    targets = [x_peer, peer(1), peer(2), peer(4), peer(8), peer(12)]
    for target in targets:
        pl.semaphore_signal(
            barrier, inc=1, device_id=target, device_id_type=pl.DeviceIdType.MESH
        )

    token = expert * own_rows + lax.broadcasted_iota(jnp.int32, (own_rows, rows), 0)

    def onehot(which):
        picked = chosen_ref[pl.ds(which, 1), :]
        return jnp.where(picked == token, 1.0, 0.0).astype(jnp.bfloat16)

    loads[0].wait()
    other_hot = onehot(other)
    own_hot = onehot(expert)

    ids = {}

    def slot_of(key):
        return ids.setdefault(key, len(ids))

    started = []
    incoming = {}

    def send(source, landing, target, key):
        number = slot_of(key)
        copy = pltpu.make_async_remote_copy(
            src_ref=source,
            dst_ref=landing,
            send_sem=send_sem.at[number],
            recv_sem=recv_sem.at[number],
            device_id=target,
            device_id_type=pl.DeviceIdType.MESH,
        )
        copy.start()
        started.append(copy)
        incoming[key] = copy

    loads[1].wait()
    xsend[0] = contract(other_hot, act_ref[...], 0, 0).astype(jnp.bfloat16)
    pl.semaphore_wait(barrier, len(targets))
    send(xsend.at[0], xrecv.at[0], x_peer, ("x", 0))
    loads[2].wait()
    xsend[1] = contract(other_hot, grad_ref[...], 0, 0).astype(jnp.bfloat16)
    send(xsend.at[1], xrecv.at[1], x_peer, ("x", 1))
    own_picks = [
        contract(own_hot, ref[...], 0, 0).astype(jnp.bfloat16)
        for ref in (act_ref, grad_ref)
    ]
    pre[...] = jnp.zeros_like(pre)
    raw[...] = jnp.zeros_like(raw)

    inner = flip(bits[2], bits[3])
    by_inner = []

    def pass_on(array, slot, landing, target, key):
        copy = pltpu.make_async_remote_copy(
            src_ref=gat.at[array, slot],
            dst_ref=gat.at[array, landing],
            send_sem=send_sem.at[slot_of(("g", array) + key)],
            recv_sem=gather_sem.at[array, landing],
            device_id=target,
            device_id_type=pl.DeviceIdType.MESH,
        )
        return copy

    def begin(copy):
        copy.start()
        started.append(copy)

    def arrived(array, slot):
        pltpu.make_async_remote_copy(
            src_ref=gat.at[array, slot],
            dst_ref=gat.at[array, slot],
            send_sem=send_sem.at[0],
            recv_sem=gather_sem.at[array, slot],
            device_id=peer(1),
            device_id_type=pl.DeviceIdType.MESH,
        ).wait_recv()

    def to_pair(array, kz, low, step):
        begin(
            pass_on(array, 4 * kz + low, 4 * kz + low + 1, peer(1), ("pair", step, low))
        )

    def to_column(array, kz, step):
        begin(
            pass_on(array, 4 * kz, 4 * kz + 2, peer(2), ("column", step))
        )

    def along_line(array, slot, landing, mask, step):
        copy = pass_on(array, slot, landing, peer(mask), ("line", step))
        by_inner.append(copy)

        @pl.when(inner == 1)
        def _():
            copy.start()

    def add_group(kz):
        base = group_of(kz)

        def body(step, carry):
            lane = flip(bits[0], step % 2) + 2 * flip(bits[1], step // 2)
            start = pl.multiple_of((4 * base + lane) * width, width)
            slot = 4 * kz + step
            pre[...] += jnp.dot(
                gat[0, slot], win_v[pl.ds(start, width), :],
                preferred_element_type=jnp.float32,
            )
            raw[...] += contract(gat[1, slot], wout_v[:, pl.ds(start, width)], 1, 1)
            return carry

        lax.fori_loop(0, 4, body, 0)

    kz_at = [0, 1, 2 + inner, 3 - inner]
    for array in range(2):
        incoming[("x", array)].wait_recv()
        gat[array, 0] = own_picks[array] + xrecv[array]
        begin(pass_on(array, 0, 4, peer(4), ("own",)))
        along_line(array, 0, 12, 12, 0)
        to_column(array, 0, 0)
        to_pair(array, 0, 0, 0)
    for load in loads[3:]:
        load.wait()
    for step in range(1, zgroups + 2):
        for array in range(2):
            if step < zgroups:
                kz = kz_at[step]
                arrived(array, 4 * kz)
                if step == 1:
                    along_line(array, 4, 8, 12, 1)
                elif step == 2:
                    along_line(array, 12, 8, 4, 2)
                else:
                    along_line(array, 8, 12, 4, 3)
                to_column(array, kz, step)
                to_pair(array, kz, 0, step)
        for array in range(2):
            if step <= zgroups:
                kz = kz_at[step - 1]
                arrived(array, 4 * kz + 2)
                to_pair(array, kz, 2, step - 1)
        if step >= 2:
            kz = kz_at[step - 2]
            for array in range(2):
                arrived(array, 4 * kz + 1)
                arrived(array, 4 * kz + 3)
            add_group(kz)

    chunk = 32
    score_col = jnp.broadcast_to(scores_ref[...], (128, rows)).T
    gate_rows[...] = score_col

    def activate(step, carry):
        span = pl.ds(pl.multiple_of(step * chunk, chunk), chunk)
        gelu_val, gelu_slope = gelu_parts(pre[span, :])
        back = raw[span, :]
        score = jnp.concatenate([gate_rows[span, :]] * (hidden_units // 128), axis=1)
        hidden = gelu_val.astype(jnp.bfloat16).astype(jnp.float32)
        product = hidden * back
        folded = product[:, :128]
        for piece in range(1, hidden_units // 128):
            folded = folded + product[:, piece * 128:(piece + 1) * 128]
        back_b[span, :] = (score * back * gelu_slope).astype(jnp.bfloat16)
        pre[span, :] = score * gelu_val
        gate_rows[span, :] = folded
        return carry

    lax.fori_loop(0, rows // chunk, activate, 0)

    def partials(kz):
        base = group_of(kz)

        def body(step, carry):
            lane = flip(bits[0], step % 2) + 2 * flip(bits[1], step // 2)
            start = pl.multiple_of((4 * base + lane) * width, width)
            part[4 * kz + step] = contract(
                back_b[...], win_v[pl.ds(start, width), :], 1, 1
            )
            return carry

        lax.fori_loop(0, 4, body, 0)
        for ky in range(2):
            place = 2 * kz + ky
            s_send[place] = part[4 * kz + 2 * ky + 1].astype(jnp.bfloat16)
            send(s_send.at[place], s_recv.at[place], peer(1), ("s", place))

    def pair_sums(kz):
        place = 2 * kz + 1
        incoming[("s", place)].wait_recv()
        y_send[kz] = (part[4 * kz + 2] + s_recv[place].astype(jnp.float32)).astype(
            jnp.bfloat16
        )
        send(y_send.at[kz], y_recv.at[kz], peer(2), ("y", kz))
        incoming[("s", place - 1)].wait_recv()
        q_keep[kz] = part[4 * kz] + s_recv[place - 1].astype(jnp.float32)

    order = (2, 3, 1, 0)
    for position, kz in enumerate(order):
        partials(kz)
        if position:
            pair_sums(order[position - 1])
    pair_sums(order[-1])

    g_send[0] = jnp.broadcast_to(
        jnp.sum(gate_rows[...].T, axis=0, keepdims=True), (8, rows)
    )
    send(g_send.at[0], g_recv.at[0], peer(1), ("gate", 0))
    hidden_t[...] = pre[...].T.astype(jnp.bfloat16)

    def weight_grads(kz):
        base = group_of(kz)

        def body(step, carry):
            lane = flip(bits[0], step % 2) + 2 * flip(bits[1], step // 2)
            start = pl.multiple_of((4 * base + lane) * width, width)
            slot = 4 * kz + step
            wing_v[pl.ds(start, width), :] = contract(
                gat[0, slot], back_b[...], 0, 0
            ).astype(jnp.bfloat16)
            woutg_v[:, pl.ds(start, width)] = jnp.dot(
                hidden_t[...], gat[1, slot], preferred_element_type=jnp.float32
            ).astype(jnp.bfloat16)
            return carry

        lax.fori_loop(0, 4, body, 0)

    weight_grads(0)
    incoming[("gate", 0)].wait_recv()
    g_send[1] = g_send[0] + g_recv[0]
    send(g_send.at[1], g_recv.at[1], peer(2), ("gate", 1))

    total = None
    for kz in order:
        incoming[("y", kz)].wait_recv()
        value = q_keep[kz] + y_recv[kz].astype(jnp.float32)
        if kz:
            z_send[kz - 1] = value.astype(jnp.bfloat16)
            send(z_send.at[kz - 1], z_recv.at[kz - 1], peer(4 * kz), ("z", kz - 1))
            if kz == order[0]:
                incoming[("gate", 1)].wait_recv()
                g_send[2] = g_send[1] + g_recv[1]
                for kg in range(1, zgroups):
                    send(g_send.at[2], g_recv.at[1 + kg], peer(4 * kg), ("gate", 1 + kg))
            weight_grads(kz)
        else:
            q_keep[0] = value
    total = q_keep[0]
    for kz in order[:-1]:
        incoming[("z", kz - 1)].wait_recv()
        total = total + z_recv[kz - 1].astype(jnp.float32)
    t_send[...] = total.astype(jnp.bfloat16)
    send(t_send, t_recv, x_peer, ("t", 0))
    for kg in range(1, zgroups):
        incoming[("gate", 1 + kg)].wait_recv()
    gate_sum = (g_send[2] + g_recv[2]) + (g_recv[3] + g_recv[4])
    gate_ref[...] = gate_sum[0:1, :]
    mine = jnp.dot(own_hot, t_send[...], preferred_element_type=jnp.float32)
    incoming[("t", 0)].wait_recv()
    theirs = jnp.dot(other_hot, t_recv[...], preferred_element_type=jnp.float32)
    actg_ref[...] = (mine + theirs).astype(jnp.bfloat16)
    for copy in started:
        copy.wait_send()

    @pl.when(inner == 1)
    def _():
        for copy in by_inner:
            copy.wait_send()


def store_kernel(*refs):
    sources, results, sems = refs[:4], refs[4:8], refs[8]
    pieces = 4
    copies = []
    for place in range(2):
        source, result = sources[place], results[place].at[0]
        step = source.shape[0] // pieces
        for piece in range(pieces):
            span = pl.ds(piece * step, step)
            copies.append((source.at[span], result.at[span]))
    copies += [(sources[place], results[place]) for place in (2, 3)]
    running = [
        pltpu.make_async_copy(source, result, sems.at[number])
        for number, (source, result) in enumerate(copies)
    ]
    for copy in running:
        copy.start()
    for copy in running:
        copy.wait()


def fused(activations, out_grad, w_in, w_out, chosen, gate_scores):
    own_rows, width = activations.shape
    _, model, hidden_units = w_in.shape
    rows = chosen.shape[1]
    copies = 64
    half, full = jnp.bfloat16, jnp.float32
    vmem = pl.BlockSpec(memory_space=pltpu.VMEM)
    in_hbm = pl.BlockSpec(memory_space=pltpu.HBM)
    results = pl.pallas_call(
        fused_kernel,
        out_shape=(
            jax.ShapeDtypeStruct((model, hidden_units), half),
            jax.ShapeDtypeStruct((hidden_units, model), half),
            jax.ShapeDtypeStruct((own_rows, width), half),
            jax.ShapeDtypeStruct((1, rows), full),
        ),
        in_specs=[in_hbm] * 6,
        out_specs=(vmem,) * 4,
        scratch_shapes=[
            pltpu.VMEM((own_rows, width), half),
            pltpu.VMEM((own_rows, width), half),
            pltpu.VMEM(chosen.shape, chosen.dtype),
            pltpu.VMEM((1, rows), full),
            pltpu.VMEM((model, hidden_units), half),
            pltpu.VMEM((hidden_units, model), half),
            pltpu.VMEM((2, 16, rows, width), half),
            pltpu.VMEM((2, rows, width), half),
            pltpu.VMEM((2, rows, width), half),
            pltpu.VMEM((rows, hidden_units), full),
            pltpu.VMEM((rows, hidden_units), full),
            pltpu.VMEM((hidden_units, rows), half),
            pltpu.VMEM((rows, hidden_units), half),
            pltpu.VMEM((rows, 128), full),
            pltpu.VMEM((16, rows, width), full),
            pltpu.VMEM((8, rows, width), half),
            pltpu.VMEM((8, rows, width), half),
            pltpu.VMEM((4, rows, width), full),
            pltpu.VMEM((4, rows, width), half),
            pltpu.VMEM((4, rows, width), half),
            pltpu.VMEM((3, rows, width), half),
            pltpu.VMEM((3, rows, width), half),
            pltpu.VMEM((rows, width), half),
            pltpu.VMEM((rows, width), half),
            pltpu.VMEM((3, 8, rows), full),
            pltpu.VMEM((5, 8, rows), full),
            pltpu.SemaphoreType.DMA((10,)),
            pltpu.SemaphoreType.DMA((copies,)),
            pltpu.SemaphoreType.DMA((copies,)),
            pltpu.SemaphoreType.DMA((2, 16)),
        ],
        compiler_params=pltpu.CompilerParams(
            collective_id=0, has_side_effects=True, vmem_limit_bytes=44 * 2**20
        ),
        cost_estimate=pl.CostEstimate(
            flops=10 * rows * model * hidden_units,
            bytes_accessed=8 * model * hidden_units,
            transcendentals=rows * hidden_units,
        ),
    )(activations, out_grad, w_in, w_out, chosen, gate_scores)
    return pl.pallas_call(
        store_kernel,
        out_shape=(
            jax.ShapeDtypeStruct((1, model, hidden_units), half),
            jax.ShapeDtypeStruct((1, hidden_units, model), half),
            jax.ShapeDtypeStruct((own_rows, width), half),
            jax.ShapeDtypeStruct((1, rows), full),
        ),
        in_specs=[vmem] * 4,
        out_specs=(in_hbm,) * 4,
        scratch_shapes=[pltpu.SemaphoreType.DMA((10,))],
        compiler_params=pltpu.CompilerParams(vmem_limit_bytes=2**20),
    )(*results)


def fits(mesh, operands):
    activations, _, w_in, _, chosen, _ = operands
    return (
        mesh.shape["dp"] == 16
        and mesh.shape["expert"] == 2
        and activations.shape[0] % 256 == 0
        and activations.shape[1] == 4096
        and w_in.shape == (2, 4096, 8192)
        and chosen.shape == (2, 256)
    )


def solution(mesh):
    def run(*operands):
        body = fused if fits(mesh, operands) else per_device
        return jax.shard_map(
            body,
            mesh=mesh,
            in_specs=(
                P("expert", "dp"),
                P("expert", "dp"),
                P("expert", None, "dp"),
                P("expert", "dp", None),
                P(),
                P("expert", None),
            ),
            out_specs=(
                P("expert", None, "dp"),
                P("expert", "dp", None),
                P("expert", "dp"),
                P("expert", None),
            ),
            check_vma=False,
        )(*operands)

    return run
```
